32 devices in a mesh: grp: 2 (over x), tile: 16 (over z, y, core).
Axes of the slice: x: 2, y: 2, z: 4, core: 2. Of those that a mesh axis runs over, the one named last changes fastest.
Arguments:
- ocean_anom: bfloat16 [1024, 80, 256], P(('grp', 'tile')), parts along dimension 0, may hold values from -6 to 6
- ocean_innov: bfloat16 [1024, 256], P(('grp', 'tile')), parts along dimension 0, may hold values from -6 to 6
- ocean_mean: float32 [1024, 256], P(('grp', 'tile')), parts along dimension 0, may hold values from -6 to 6
- atm_anom: bfloat16 [1024, 80, 256], P(('grp', 'tile')), parts along dimension 0, may hold values from -6 to 6
- atm_innov: bfloat16 [1024, 256], P(('grp', 'tile')), parts along dimension 0, may hold values from -6 to 6
- atm_mean: float32 [1024, 256], P(('grp', 'tile')), parts along dimension 0, may hold values from -6 to 6
- air_temp: float32 [512, 512], P(('grp', 'tile')), parts along dimension 0, may hold values from -6 to 6
- pair_owner: int32 [2048, 1], P('tile'), may hold values from 0 to 15; in each aligned block of 128 rows (0 to 127, 128 to 255, ...) at most 12 rows name the same one
- pair_slot: int32 [2048], P('tile'), may hold values from 0 to 31
- pair_ocean: int32 [2048], P('tile'), may hold values from 0 to 31
- pair_shift: int32 [2048, 2], P('tile'), may hold values from -8 to 8
Outputs:
- atm_analysis: float32 [1024, 256], P(('grp', 'tile')), parts along dimension 0
- ocean_next: float32 [512, 512], P(('grp', 'tile')), parts along dimension 0
The draws below stay inside these ranges and needn't reach their ends.
There are 2 independent parts, one for each index of `grp`. The reference program is written for one: setup_inputs(seed, part) draws one part's arguments, and reference() takes and returns one part's arrays. A program takes and returns all parts, laid end to end along the dimension named above; an argument that names none is the same for every part. Nothing has to cross between parts.
Inputs may be any that keep to these rules, and one draw needn't show every extreme that they name: `pair_owner`: in the rows of one device no device number appears more than 12 times, and some device number appears exactly 12 times.
All inputs are finite; a program needn't handle non-finite values.
Results may differ from the reference program's by a relative error of at most 0.0003.
The reference program's roundings to bfloat16 on the way count: a program that leaves them out, or rounds other values in their place, can miss the bound.
Values may be sent and summed in bfloat16 or wider, within the bound.
A program may use at most 128 MiB of HBM per device.

```python
import math
import jax
import jax.numpy as jnp
import numpy as np
from jax import lax

K = 80
SIDE = 16
OT = 32
RADIUS = 4
SHIFT_MAX = 8
CELLS = 256
PD = 128
MOST = 12
NO = 512
NP = 2048
NXO = 256
NYO = 512
N_TILE = 16


def member_mode(key, strength):
    signs = jnp.where(jax.random.bernoulli(key, 0.5, (K,)), 1.0, -1.0).astype(jnp.float32)
    return strength * signs[None, :, None]


def draw_ocean_anom(key, part):
    common = member_mode(key, 0.3)
    key = jax.random.fold_in(key, 3)
    noise = jax.random.truncated_normal(key, -5.5, 5.5, (NO, K, CELLS), jnp.float32)
    return (common + noise).astype(jnp.bfloat16)


def draw_atm_anom(key, part):
    common = member_mode(key, 0.3)
    key = jax.random.fold_in(key, 5)
    noise = jax.random.truncated_normal(key, -5.5, 5.5, (NO, K, CELLS), jnp.float32)
    return (common + noise).astype(jnp.bfloat16)


def draw_ocean_innov(key, part):
    key = jax.random.fold_in(key, 7)
    values = jax.random.truncated_normal(key, -6.0, 6.0, (NO, CELLS), jnp.float32)
    return values.astype(jnp.bfloat16)


def draw_atm_innov(key, part):
    key = jax.random.fold_in(key, 11)
    values = jax.random.truncated_normal(key, -6.0, 6.0, (NO, CELLS), jnp.float32)
    return values.astype(jnp.bfloat16)


def draw_ocean_mean(key, part):
    key = jax.random.fold_in(key, 13)
    values = jax.random.truncated_normal(key, -6.0, 6.0, (NO, CELLS), jnp.float32)
    return values.astype(jnp.float32)


def draw_atm_mean(key, part):
    key = jax.random.fold_in(key, 17)
    values = jax.random.truncated_normal(key, -6.0, 6.0, (NO, CELLS), jnp.float32)
    return values.astype(jnp.float32)


def set_ends(values, rng, smallest, top_value):
    spot = [jax.random.randint(jax.random.fold_in(rng, axis), (), 0, length) for axis, length in enumerate(values.shape)]
    longest = values.shape.index(max(values.shape))
    next_to = spot[:longest] + [(spot[longest] + 1) % values.shape[longest]] + spot[longest + 1:]
    return values.at[tuple(spot)].set(smallest).at[tuple(next_to)].set(top_value)


def block_levels(rng, extent, cuts, least, largest):
    level, own = 1.0, jax.random.fold_in(rng, 6)
    for dim, parts in cuts:
        steps = jnp.exp(jax.random.uniform(jax.random.fold_in(own, dim), (parts,), jnp.float32, least / len(cuts), largest / len(cuts)))
        level = level * jnp.repeat(steps, extent[dim] // parts).reshape([-1 if axis == dim else 1 for axis in range(len(extent))])
    return level


def deal_out(key, own, number, rows, count, top, reach, slope):
    ranking = jax.random.permutation(key, count)
    heavy_load, ordinary = portions_of(count, rows * top, reach, slope, True), portions_of(count, rows * top, reach, slope, False)
    places = jnp.arange(count)

    def named(lengths, rotation):
        used = int((lengths > 0).sum())
        fixed = max(1, used // 4)
        passed = fixed + (places - fixed + rotation * (used - fixed)) % max(1, count - fixed)
        return jnp.zeros((count,), jnp.int32).at[ranking[jnp.where(places < fixed, places, passed)]].set(jnp.asarray(lengths, jnp.int32))

    lengths = jnp.where(number % 4 == 0, named(heavy_load, number // 4), named(ordinary, number - number // 4 - 1))
    mixed = jax.random.permutation(jax.random.fold_in(own, 3), count)
    donor, taker = mixed[0:count // 2 * 2:2], mixed[1:count // 2 * 2:2]
    slack = jnp.minimum(lengths[donor] - 1, reach - lengths[taker]) // 2
    slack = jnp.where((donor == ranking[0]) | (taker == ranking[0]) | (lengths[taker] == 0), 0, jnp.maximum(slack, 0))
    passed = jax.random.randint(jax.random.fold_in(own, 4), (count // 2,), 0, 1 << 20) % (slack + 1)
    lengths = lengths.at[donor].add(-passed).at[taker].add(passed)
    items = jnp.searchsorted(jnp.cumsum(lengths), jnp.arange(rows * top), side="right").astype(jnp.int32)
    listing = items.reshape(top, rows).T
    listing = listing[jax.random.permutation(jax.random.fold_in(own, 1), rows)]
    rotation = jax.random.randint(jax.random.fold_in(own, 2), (rows, 1), 0, top)
    return jnp.take_along_axis(listing, (jnp.arange(top)[None, :] + rotation) % top, axis=1)


def portions_of(number_of, total, reach, lean, full):
    loads = [(1 << 20) // math.isqrt(rank ** lean) + 1 for rank in range(1, number_of + 1)]
    largest = reach if full else min(reach, max(-(-total // number_of), total * loads[0] // sum(loads)))
    least = 1 if total - largest >= number_of - 1 else 0
    counts, spare = [largest] + [least] * (number_of - 1), total - largest - least * (number_of - 1)
    while spare > 0:
        movable = [i for i in range(1, number_of) if counts[i] < largest] or [i for i in range(1, number_of) if counts[i] < reach]
        pool, budget = sum([loads[i] for i in movable]), spare
        for i in movable:
            extra = min(reach - counts[i], max(1, budget * loads[i] // pool), spare)
            counts[i] = counts[i] + extra
            spare = spare - extra
    return np.array(counts)


def gaussian(rng, shape, deviation, most, split=(), kind=jnp.bfloat16):
    array = jax.random.normal(rng, shape, jnp.float32) * deviation
    if len(split) > 0:
        array = block_levels(rng, shape, split, -0.22, 0.18) * array
    return jnp.clip(array, min=-most, max=most).astype(kind)


def setup_inputs(seed: int = 0, part: int = 0) -> dict:
    streams_of = jax.random.split(jax.random.key(seed), 12)
    own_keys = jax.random.split(jax.random.fold_in(streams_of[11], part), 12)
    ocean_anom = draw_ocean_anom(jax.random.fold_in(jax.random.fold_in(streams_of[11], part), 71), part)
    ocean_innov = draw_ocean_innov(jax.random.fold_in(jax.random.fold_in(streams_of[11], part), 71), part)
    ocean_mean = draw_ocean_mean(jax.random.fold_in(jax.random.fold_in(streams_of[11], part), 71), part)
    atm_anom = draw_atm_anom(jax.random.fold_in(jax.random.fold_in(streams_of[11], part), 71), part)
    atm_innov = draw_atm_innov(jax.random.fold_in(jax.random.fold_in(streams_of[11], part), 71), part)
    atm_mean = draw_atm_mean(jax.random.fold_in(jax.random.fold_in(streams_of[11], part), 71), part)
    air_temp = gaussian(own_keys[6], (NXO, NYO), 1.0, 6.0, ((0, 16),), jnp.float32)
    pair_owner_keys = jax.random.split(jax.random.fold_in(streams_of[7], 1), NP // PD)
    pair_owner_turns = jax.random.permutation(jax.random.fold_in(streams_of[7], 3), NP // PD)
    pair_owner = jax.vmap(lambda own, number: deal_out(jax.random.fold_in(streams_of[7], 2), own, number, PD, N_TILE, 1, MOST, 2))(pair_owner_keys, pair_owner_turns).reshape((NP, 1))
    pair_slot = set_ends(jax.random.randint(streams_of[8], (NP,), 0, OT), jax.random.fold_in(streams_of[8], 1), 0, OT - 1).astype(jnp.int32)
    pair_ocean = set_ends(jax.random.randint(streams_of[9], (NP,), 0, OT), jax.random.fold_in(streams_of[9], 1), 0, OT - 1).astype(jnp.int32)
    pair_shift = set_ends(jax.random.randint(streams_of[10], (NP, 2), -SHIFT_MAX, SHIFT_MAX + 1), jax.random.fold_in(streams_of[10], 1), -SHIFT_MAX, SHIFT_MAX).astype(jnp.int32)
    return {"ocean_anom": ocean_anom, "ocean_innov": ocean_innov, "ocean_mean": ocean_mean, "atm_anom": atm_anom, "atm_innov": atm_innov, "atm_mean": atm_mean, "air_temp": air_temp, "pair_owner": pair_owner, "pair_slot": pair_slot, "pair_ocean": pair_ocean, "pair_shift": pair_shift}


diffusion_rate = 0.2
relax_rate = 0.25

def taper_table(shift_x, shift_y):
    cell_index = jnp.arange(SIDE * SIDE, dtype=jnp.int32)
    column = cell_index // SIDE
    row_index = cell_index % SIDE
    delta_x = (column[:, None] + shift_x - column[None, :]).astype(jnp.float32)
    delta_y = (row_index[:, None] + shift_y - row_index[None, :]).astype(jnp.float32)
    radius = jnp.sqrt(delta_x * delta_x + delta_y * delta_y) / RADIUS
    inner_part = (((-0.25 * radius + 0.5) * radius + 0.625) * radius - 5.0 / 3.0) * radius * radius + 1.0
    safe_radius = jnp.maximum(radius, 1.0)
    outer_part = ((((safe_radius / 12.0 - 0.5) * safe_radius + 0.625) * safe_radius + 5.0 / 3.0) * safe_radius - 5.0) * safe_radius + 4.0 - 2.0 / (3.0 * safe_radius)
    weight = jnp.where(radius <= 1.0, inner_part, jnp.where(radius < 2.0, outer_part, 0.0))
    return weight.astype(jnp.bfloat16)

def scaled(anomalies, innovation):
    return (anomalies.astype(jnp.float32) * innovation.astype(jnp.float32)[..., None, :]).astype(jnp.bfloat16)

def self_term(anomalies, weighted, table):
    members = anomalies.shape[1]
    towards = jnp.dot(weighted.reshape(-1, table.shape[0]), table, preferred_element_type=jnp.float32)
    towards = towards.reshape(anomalies.shape)
    return lax.optimization_barrier(jnp.sum(anomalies.astype(jnp.float32) * towards, axis=1)) / (members - 1)

def cross_terms(ocean_part, ocean_weighted, atm_part, atm_weighted, tables):
    members = ocean_part.shape[1]
    towards_ocean = jnp.einsum('bki,bij->bkj', atm_weighted.astype(jnp.float32), tables.astype(jnp.float32))
    ocean_terms = lax.optimization_barrier(jnp.sum(ocean_part.astype(jnp.float32) * towards_ocean, axis=1)) / (members - 1)
    towards_atm = jnp.einsum('bkj,bij->bki', ocean_weighted.astype(jnp.float32), tables.astype(jnp.float32))
    atm_terms = lax.optimization_barrier(jnp.sum(atm_part.astype(jnp.float32) * towards_atm, axis=1)) / (members - 1)
    return (ocean_terms, atm_terms)

def reference(ocean_anom, ocean_innov, ocean_mean, atm_anom, atm_innov, atm_mean, air_temp, pair_owner, pair_slot, pair_ocean, pair_shift):
    cell_total = SIDE * SIDE
    ocean_scaled = scaled(ocean_anom, ocean_innov)
    atm_scaled = scaled(atm_anom, atm_innov)
    self_table = taper_table(jnp.int32(0), jnp.int32(0))
    ocean_inc = self_term(ocean_anom, ocean_scaled, self_table)
    atm_inc = self_term(atm_anom, atm_scaled, self_table)
    pair_total = pair_slot.shape[0]
    per_device = pair_total // N_TILE
    position = jnp.arange(pair_total, dtype=jnp.int32)
    ocean_index = (position // per_device * OT + pair_ocean).astype(jnp.int32)
    atm_index = (pair_owner[:, 0] * OT + pair_slot).astype(jnp.int32)

    def one_block(block_items):
        ocean_rows, atm_rows, shifts = block_items
        tables = jax.vmap(taper_table)(shifts[:, 0], shifts[:, 1])
        return cross_terms(ocean_anom[ocean_rows], ocean_scaled[ocean_rows], atm_anom[atm_rows], atm_scaled[atm_rows], tables)
    ocean_pairs, atm_pairs = lax.map(one_block, (ocean_index.reshape(N_TILE, per_device), atm_index.reshape(N_TILE, per_device), pair_shift.reshape(N_TILE, per_device, 2)))
    ocean_inc = ocean_inc.at[ocean_index].add(ocean_pairs.reshape(pair_total, cell_total))
    atm_inc = atm_inc.at[atm_index].add(atm_pairs.reshape(pair_total, cell_total))
    atm_analysis = atm_mean + atm_inc
    ocean_grid = (ocean_mean + ocean_inc).reshape(N_TILE, OT, SIDE, SIDE).transpose(0, 2, 1, 3).reshape(N_TILE * SIDE, OT * SIDE)
    padded = jnp.pad(ocean_grid, ((0, 0), (1, 1)), mode='edge')
    laplace = jnp.roll(ocean_grid, 1, 0) + jnp.roll(ocean_grid, -1, 0) + padded[:, 2:] + padded[:, :-2] - 4.0 * ocean_grid
    ocean_next = ocean_grid + diffusion_rate * laplace + relax_rate * (air_temp - ocean_grid)
    return (atm_analysis, ocean_next)
```

```python
import jax
import jax.numpy as jnp
from jax import lax
from jax.experimental import pallas as pl
from jax.experimental.pallas import tpu as pltpu
from jax.sharding import PartitionSpec as P

SIDE = 16
RADIUS = 4


diffusion_rate = 0.2
relax_rate = 0.25


def padded_2(shard, sides, width):
    for axis, dim in sides:
        peers, length = (lax.axis_size(axis), shard.shape[dim])
        up = [(i, (i + 1) % peers) for i in range(peers)]
        down = [(j, i) for i, j in up]
        last = lax.slice_in_dim(shard, length - width, length, axis=dim)
        initial = lax.slice_in_dim(shard, 0, width, axis=dim)
        before = lax.ppermute(last, axis, up)
        after = lax.ppermute(initial, axis, down)
        shard = jnp.concatenate([before, shard, after], axis=dim)
    return shard


SHIFT_MAX = 8


def taper_table(shift_x, shift_y):
    cell_index = jnp.arange(SIDE * SIDE, dtype=jnp.int32)
    column = cell_index // SIDE
    row_index = cell_index % SIDE
    delta_x = (column[:, None] + shift_x - column[None, :]).astype(jnp.float32)
    delta_y = (row_index[:, None] + shift_y - row_index[None, :]).astype(jnp.float32)
    return taper(delta_x, delta_y)


def taper_strips():
    rows = jnp.arange((SIDE + 2 * SHIFT_MAX) * SIDE, dtype=jnp.int32)[None, :, None]
    cols = jnp.arange(SIDE * SIDE, dtype=jnp.int32)[None, None, :]
    sy = jnp.arange(2 * SHIFT_MAX + 1, dtype=jnp.int32)[:, None, None] - SHIFT_MAX
    delta_x = (rows // SIDE - SHIFT_MAX - cols // SIDE + 0 * sy).astype(jnp.float32)
    delta_y = (rows % SIDE + sy - cols % SIDE).astype(jnp.float32)
    return taper(delta_x, delta_y)


def taper(delta_x, delta_y):
    radius = jnp.sqrt(delta_x * delta_x + delta_y * delta_y) / RADIUS
    inner_part = (
        ((-0.25 * radius + 0.5) * radius + 0.625) * radius - 5.0 / 3.0
    ) * radius * radius + 1.0
    safe_radius = jnp.maximum(radius, 1.0)
    outer_part = (
        (
            (((safe_radius / 12.0 - 0.5) * safe_radius + 0.625) * safe_radius + 5.0 / 3.0)
            * safe_radius
            - 5.0
        )
        * safe_radius
        + 4.0
        - 2.0 / (3.0 * safe_radius)
    )
    weight = jnp.where(radius <= 1.0, inner_part, jnp.where(radius < 2.0, outer_part, 0.0))
    return weight.astype(jnp.bfloat16)


def scaled(anomalies, innovation):
    return (anomalies.astype(jnp.float32) * innovation.astype(jnp.float32)[..., None, :]).astype(
        jnp.bfloat16
    )


def self_term(anomalies, weighted, table):
    members = anomalies.shape[1]
    towards = jnp.dot(
        weighted.reshape(-1, table.shape[0]), table, preferred_element_type=jnp.float32
    )
    towards = towards.reshape(anomalies.shape)
    return jnp.sum(anomalies.astype(jnp.float32) * towards, axis=1) / (members - 1)


GROUP = 8


def pair_kernel(asked, anom, innov, atm, atm_scaled, strips, ocean_out, atm_out):
    step = pl.program_id(0)
    members = anom.shape[1]
    cells = SIDE * SIDE
    for g in range(GROUP):
        base = (step * GROUP + g) * 4
        slot = asked[base + 1]
        sx = asked[base + 2]
        sy = asked[base + 3]
        there = strips[sy + SHIFT_MAX, pl.ds(pl.multiple_of((sx + SHIFT_MAX) * SIDE, SIDE), cells), :]
        back = strips[SHIFT_MAX - sy, pl.ds(pl.multiple_of((SHIFT_MAX - sx) * SIDE, SIDE), cells), :]
        ocean = anom[g].astype(jnp.float32)
        ocean_scaled = (ocean * innov[g : g + 1, :]).astype(jnp.bfloat16)
        towards = jnp.dot(atm_scaled[slot], there, preferred_element_type=jnp.float32)
        ocean_out[g : g + 1, :] = jnp.sum(ocean * towards, axis=0, keepdims=True) / (members - 1)
        towards = jnp.dot(ocean_scaled, back, preferred_element_type=jnp.float32)
        atm_part = atm[slot].astype(jnp.float32)
        atm_out[g : g + 1, :] = jnp.sum(atm_part * towards, axis=0, keepdims=True) / (members - 1)


def pair_terms(asked, anom, innov, atm, atm_scaled, strips):
    slots, members, cells = anom.shape
    whole = lambda i, q: (0, 0, 0)
    row = pl.BlockSpec((GROUP, cells), lambda i, q: (i, 0))
    return pl.pallas_call(
        pair_kernel,
        grid_spec=pltpu.PrefetchScalarGridSpec(
            num_scalar_prefetch=1,
            grid=(slots // GROUP,),
            in_specs=[
                pl.BlockSpec((GROUP, members, cells), lambda i, q: (i, 0, 0)),
                row,
                pl.BlockSpec(atm.shape, whole),
                pl.BlockSpec(atm.shape, whole),
                pl.BlockSpec(strips.shape, whole),
            ],
            out_specs=[row, row],
        ),
        out_shape=[jax.ShapeDtypeStruct((slots, cells), jnp.float32)] * 2,
        compiler_params=pltpu.CompilerParams(vmem_limit_bytes=40 * 2**20),
    )(asked.reshape(-1), anom, innov.astype(jnp.float32), atm, atm_scaled, strips)


def local(
    ocean_anom,
    ocean_innov,
    ocean_mean,
    atm_anom,
    atm_innov,
    atm_mean,
    air_temp,
    pair_owner,
    pair_slot,
    pair_ocean,
    pair_shift,
):
    peers = lax.axis_size("tile")
    listed_pairs = pair_slot.shape[0]
    capacity = max(2, 3 * listed_pairs // (2 * peers))
    slot_total = peers * capacity
    members = ocean_anom.shape[1]
    cell_total = ocean_anom.shape[2]
    ocean_tiles = ocean_anom.shape[0]
    ocean_scaled = scaled(ocean_anom, ocean_innov)
    atm_scaled = scaled(atm_anom, atm_innov)
    self_table = taper_table(jnp.int32(0), jnp.int32(0))
    ocean_inc = self_term(ocean_anom, ocean_scaled, self_table)
    atm_inc = self_term(atm_anom, atm_scaled, self_table)
    owners = pair_owner[:, 0]
    position = jnp.arange(listed_pairs, dtype=jnp.int32)
    earlier = (owners[:, None] == owners[None, :]) & (position[None, :] < position[:, None])
    slot_index = owners * capacity + jnp.sum(earlier, axis=1)
    request_rows = jnp.stack(
        [jnp.ones_like(owners), pair_slot, pair_shift[:, 0], pair_shift[:, 1]], axis=1
    )
    request = jnp.zeros((slot_total, 4), jnp.int32).at[slot_index].set(request_rows)
    arrived = lax.all_to_all(request, "tile", split_axis=0, concat_axis=0, tiled=True)
    slot_live = (arrived[:, 0] == 1).astype(jnp.float32)
    asked_tiles = arrived[:, 1]
    shipped = (
        jnp.zeros((slot_total, members, cell_total), jnp.bfloat16)
        .at[slot_index]
        .set(ocean_anom[pair_ocean])
    )
    shipped_innov = (
        jnp.zeros((slot_total, cell_total), jnp.bfloat16)
        .at[slot_index]
        .set(ocean_innov[pair_ocean])
    )
    got_anom, got_innov = (
        lax.all_to_all(shipped, "tile", split_axis=0, concat_axis=0, tiled=True),
        lax.all_to_all(shipped_innov, "tile", split_axis=0, concat_axis=0, tiled=True),
    )

    ocean_terms, atm_terms = pair_terms(
        arrived, got_anom, got_innov, atm_anom, atm_scaled, taper_strips()
    )
    atm_inc = atm_inc.at[asked_tiles].add(
        atm_terms.reshape(slot_total, cell_total) * slot_live[:, None]
    )
    returned = lax.all_to_all(
        ocean_terms.reshape(slot_total, cell_total), "tile", split_axis=0, concat_axis=0, tiled=True
    )
    ocean_inc = ocean_inc.at[pair_ocean].add(returned[slot_index])
    atm_analysis = atm_mean + atm_inc
    side_cells = air_temp.shape[0]
    ocean_grid = (
        (ocean_mean + ocean_inc)
        .reshape(ocean_tiles, side_cells, side_cells)
        .transpose(1, 0, 2)
        .reshape(side_cells, ocean_tiles * side_cells)
    )
    extended = padded_2(ocean_grid, (("tile", 0),), 1)
    padded = jnp.pad(extended, ((0, 0), (1, 1)), mode="edge")
    laplace = (
        padded[2:, 1:-1]
        + padded[:-2, 1:-1]
        + padded[1:-1, 2:]
        + padded[1:-1, :-2]
        - 4.0 * ocean_grid
    )
    ocean_next = ocean_grid + diffusion_rate * laplace + relax_rate * (air_temp - ocean_grid)
    return (atm_analysis, ocean_next)


def solution(mesh):
    return jax.shard_map(
        local,
        mesh=mesh,
        in_specs=(
            P(("grp", "tile"), None, None),
            P(("grp", "tile"), None),
            P(("grp", "tile"), None),
            P(("grp", "tile"), None, None),
            P(("grp", "tile"), None),
            P(("grp", "tile"), None),
            P(("grp", "tile"), None),
            P("tile", None),
            P("tile"),
            P("tile"),
            P("tile", None),
        ),
        out_specs=(P(("grp", "tile"), None), P(("grp", "tile"), None)),
        check_vma=False,
    )
```
